32 devices in a mesh: groups: 2 (over y), dap: 4 (over z), chan: 2 (over x), sub: 2 (over core).
Axes of the slice: x: 2, y: 2, z: 4, core: 2. Of those that a mesh axis runs over, the one named last changes fastest.
Arguments:
- pair_input: bfloat16 [768, 384, 128], P(('groups', 'dap'), ('chan', 'sub')), parts along dimension 0, may hold values from -6 to 6
- first_gain: float32 [128], replicated, may hold values from 0.25 to 1.75
- first_project: bfloat16 [128, 512], replicated, may hold values from -0.5 to 0.5
- first_gate: bfloat16 [128, 128], replicated, may hold values from -0.5 to 0.5
- first_norm: float32 [128], replicated, may hold values from 0.25 to 1.75
- first_final: bfloat16 [128, 128], replicated, may hold values from -0.5 to 0.5
- second_gain: float32 [128], replicated, may hold values from 0.25 to 1.75
- second_project: bfloat16 [128, 512], replicated, may hold values from -0.5 to 0.5
- second_gate: bfloat16 [128, 128], replicated, may hold values from -0.5 to 0.5
- second_norm: float32 [128], replicated, may hold values from 0.25 to 1.75
- second_final: bfloat16 [128, 128], replicated, may hold values from -0.5 to 0.5
Outputs:
- pair_output: bfloat16 [768, 384, 128], P(('groups', 'dap'), ('chan', 'sub')), parts along dimension 0
The draws below stay inside these ranges and needn't reach their ends.
There are 2 independent parts, one for each index of `groups`. The reference program is written for one: setup_inputs(seed, part) draws one part's arguments, and reference() takes and returns one part's arrays. A program takes and returns all parts, laid end to end along the dimension named above; an argument that names none is the same for every part. Nothing has to cross between parts.
All inputs are finite; a program needn't handle non-finite values.
Results may differ from the reference program's by a relative error of at most 0.013.
Values may be sent and summed in bfloat16 or wider, within the bound.
A program may use at most 64 MiB of HBM per device.

```python
import jax
import jax.numpy as jnp
from jax import lax

C = 128
N = 384


def block_levels(key, extent, shards, least, top_value):
    def one(position, blocks):
        draws = jax.random.uniform(jax.random.fold_in(jax.random.fold_in(key, 6), position), (blocks,), jnp.float32, least / len(shards), top_value / len(shards))
        return jnp.repeat(jnp.exp(draws), extent[position] // blocks).reshape((-1,) + (1,) * (len(extent) - position - 1))

    level = one(*shards[0])
    for cut in shards[1:]:
        level = level * one(*cut)
    return level


def noise(stream_key, shape, width, limit, pieces=(), held_as=jnp.bfloat16):
    drawn = jax.random.normal(stream_key, shape, jnp.float32) * width
    if len(pieces) > 0:
        drawn = block_levels(stream_key, shape, pieces, -0.22, 0.18) * drawn
    return jnp.clip(drawn, min=-limit, max=limit).astype(held_as)


def setup_inputs(seed: int = 0, part: int = 0) -> dict:
    splits = jax.random.split(jax.random.key(seed), 12)
    part_keys = jax.random.split(jax.random.fold_in(splits[11], part), 12)
    return {
        "pair_input": noise(part_keys[0], (N, N, C), 1.0, 6.0, ((0, 4), (1, 4))),
        "first_gain": jnp.clip(1.0 + 0.15 * jax.random.normal(splits[1], (C,), jnp.float32), 0.25, 1.75),
        "first_project": noise(splits[2], (C, 4 * C), C ** -0.5, 0.5),
        "first_gate": noise(splits[3], (C, C), C ** -0.5, 0.5),
        "first_norm": jnp.clip(1.0 + 0.15 * jax.random.normal(splits[4], (C,), jnp.float32), 0.25, 1.75),
        "first_final": noise(splits[5], (C, C), C ** -0.5, 0.5),
        "second_gain": jnp.clip(1.0 + 0.15 * jax.random.normal(splits[6], (C,), jnp.float32), 0.25, 1.75),
        "second_project": noise(splits[7], (C, 4 * C), C ** -0.5, 0.5),
        "second_gate": noise(splits[8], (C, C), C ** -0.5, 0.5),
        "second_norm": jnp.clip(1.0 + 0.15 * jax.random.normal(splits[9], (C,), jnp.float32), 0.25, 1.75),
        "second_final": noise(splits[10], (C, C), C ** -0.5, 0.5),
    }


epsilon = 1e-05

def layer_norm(values, norm_gain, reduce_axis):
    average = lax.optimization_barrier(jnp.mean(values, axis=reduce_axis, keepdims=True))
    centred = values - average
    variance = lax.optimization_barrier(jnp.mean(centred * centred, axis=reduce_axis, keepdims=True))
    return centred * lax.rsqrt(variance + epsilon) * norm_gain

def project_all(pair_state, norm_gain, project, gate_matrix):
    flattened = pair_state.reshape(N * N, C).astype(jnp.float32)
    normed = layer_norm(flattened, norm_gain, 1).astype(jnp.bfloat16)
    first_half = jnp.dot(normed, project[:, :2 * C], preferred_element_type=jnp.float32)
    left_part = (jax.nn.sigmoid(first_half[:, :C]) * first_half[:, C:]).astype(jnp.bfloat16)
    second_half = jnp.dot(normed, project[:, 2 * C:], preferred_element_type=jnp.float32)
    right_part = (jax.nn.sigmoid(second_half[:, :C]) * second_half[:, C:]).astype(jnp.bfloat16)
    gating = jax.nn.sigmoid(jnp.dot(normed, gate_matrix, preferred_element_type=jnp.float32))
    return (left_part.T.reshape(C, N, N), right_part.T.reshape(C, N, N), gating)

def finish(pair_state, mixture, gating, out_gain, final_matrix):
    flattened = mixture.reshape(C, N * N).astype(jnp.float32)
    normed = layer_norm(flattened, out_gain[:, None], 0).astype(jnp.bfloat16)
    update = jnp.dot(normed.T, final_matrix, preferred_element_type=jnp.float32)
    result = pair_state.reshape(N * N, C).astype(jnp.float32) + gating * update
    return result.astype(jnp.bfloat16).reshape(N, N, C)

def reference(pair_input, first_gain, first_project, first_gate, first_norm, first_final, second_gain, second_project, second_gate, second_norm, second_final):
    left_part, right_part, gating = project_all(pair_input, first_gain, first_project, first_gate)
    mixture = jnp.einsum('cik,cjk->cij', left_part.astype(jnp.float32), right_part.astype(jnp.float32)).astype(jnp.bfloat16)
    middle = finish(pair_input, mixture, gating, first_norm, first_final)
    left_part, right_part, gating = project_all(middle, second_gain, second_project, second_gate)
    mixture = jnp.einsum('cki,ckj->cij', left_part.astype(jnp.float32), right_part.astype(jnp.float32)).astype(jnp.bfloat16)
    return finish(middle, mixture, gating, second_norm, second_final)
```

```python
import functools

import jax
import jax.numpy as jnp
from jax import lax
from jax.experimental import pallas as pl
from jax.experimental.pallas import tpu as pltpu
from jax.sharding import PartitionSpec as P

epsilon = 1e-05


def layer_norm(values, norm_gain, reduce_axis):
    average = jnp.mean(values, axis=reduce_axis, keepdims=True)
    centred = values - average
    variance = jnp.mean(centred * centred, axis=reduce_axis, keepdims=True)
    return centred * lax.rsqrt(variance + epsilon) * norm_gain


def project_in(pair_state, norm_gain, project, gate_matrix):
    row_count, col_count, features = pair_state.shape
    flattened = pair_state.reshape(row_count * col_count, features).astype(jnp.float32)
    normed = layer_norm(flattened, norm_gain, 1).astype(jnp.bfloat16)
    projected = jnp.einsum("xc,cd->dx", normed, project, preferred_element_type=jnp.float32)
    left_part = jax.nn.sigmoid(projected[:features]) * projected[features : 2 * features]
    right_part = jax.nn.sigmoid(projected[2 * features : 3 * features]) * projected[3 * features :]
    left_part = left_part.astype(jnp.bfloat16).reshape(features, row_count, col_count)
    right_part = right_part.astype(jnp.bfloat16).reshape(features, row_count, col_count)
    gating = jax.nn.sigmoid(jnp.dot(normed, gate_matrix, preferred_element_type=jnp.float32))
    return (left_part, right_part, gating)


def finish(pair_state, mixture, gating, out_gain, final_matrix):
    features = mixture.shape[0]
    flattened = mixture.reshape(features, -1).astype(jnp.float32)
    normed = layer_norm(flattened, out_gain[:, None], 0).astype(jnp.bfloat16)
    update = jnp.einsum("cx,cd->xd", normed, final_matrix, preferred_element_type=jnp.float32)
    result = pair_state.reshape(-1, features).astype(jnp.float32) + gating * update
    return result.astype(jnp.bfloat16).reshape(pair_state.shape)


def exchange_kernel(plan, sizes, *refs):
    halves, inner, chans, subs = sizes
    cols = chans * subs
    block = inner * cols
    count = len(plan)
    sources, targets = refs[:count], refs[count : 2 * count]
    sems = refs[2 * count : 5 * count]
    row = lax.axis_index("dap")
    col = lax.axis_index("chan") * subs + lax.axis_index("sub")
    mine = lax.rem(row, inner) * cols + col
    half = row // inner
    whole = halves * block
    me = row * cols + col

    def place(q):
        owner_row, owner_col = q // cols, lax.rem(q, cols)
        return {"dap": owner_row, "chan": owner_col // subs, "sub": lax.rem(owner_col, subs)}

    barrier = pltpu.get_barrier_semaphore()
    everyone = any(spans for _, spans in plan)
    reach = whole if everyone else block
    for off in range(1, reach):
        q = lax.rem(me + off, whole) if everyone else half * block + lax.rem(mine + off, block)
        pl.semaphore_signal(barrier, inc=1, device_id=place(q), device_id_type=pl.DeviceIdType.MESH)
    pl.semaphore_wait(barrier, reach - 1)

    started = []
    for off in range(0, reach):
        for (varies, spans), source, target, (sent, got, kept) in zip(
            plan, sources, targets, [sems[3 * n : 3 * n + 3] for n in range(count)]
        ):
            if spans:
                q = lax.rem(me + off, whole)
                slot, back = me, lax.rem(me - off + whole, whole)
            elif off < block:
                q = half * block + lax.rem(mine + off, block)
                slot, back = mine, lax.rem(mine - off + block, block)
            else:
                continue
            piece = source.at[q if varies else lax.rem(q, block)]
            if off == 0:
                copy = pltpu.make_async_copy(piece, target.at[slot], kept)
                copy.start()
                started.append((copy, None))
                continue
            copy = pltpu.make_async_remote_copy(
                src_ref=piece,
                dst_ref=target.at[slot],
                send_sem=sent.at[off],
                recv_sem=got.at[off],
                device_id=place(q),
                device_id_type=pl.DeviceIdType.MESH,
            )
            copy.start()
            arriving = pltpu.make_async_remote_copy(
                src_ref=piece,
                dst_ref=target.at[back],
                send_sem=sent.at[off],
                recv_sem=got.at[off],
                device_id=place(q),
                device_id_type=pl.DeviceIdType.MESH,
            )
            started.append((copy, arriving))
    for copy, arriving in started:
        if arriving is None:
            copy.wait()
        else:
            copy.wait_send()
            arriving.wait_recv()


def exchange(plan, sizes, number, *arrays):
    halves, inner, chans, subs = sizes
    block = inner * chans * subs
    shapes, sems = [], []
    for (varies, spans), array in zip(plan, arrays):
        slots = halves * block if spans else block
        shapes.append(jax.ShapeDtypeStruct((slots,) + array.shape[1:], array.dtype))
        sems += [
            pltpu.SemaphoreType.DMA((slots,)),
            pltpu.SemaphoreType.DMA((slots,)),
            pltpu.SemaphoreType.DMA,
        ]
    return pl.pallas_call(
        functools.partial(exchange_kernel, plan, sizes),
        out_shape=shapes,
        in_specs=[pl.BlockSpec(memory_space=pl.ANY)] * len(arrays),
        out_specs=[pl.BlockSpec(memory_space=pl.ANY)] * len(arrays),
        scratch_shapes=sems,
        compiler_params=pltpu.CompilerParams(collective_id=number, has_side_effects=True),
    )(*arrays)


def direct_shards(
    sizes,
    pair_input,
    first_gain,
    first_project,
    first_gate,
    first_norm,
    first_final,
    second_gain,
    second_project,
    second_gate,
    second_norm,
    second_final,
):
    halves, inner, chans, subs = sizes
    cols = chans * subs
    block = inner * cols
    rows, width, features = pair_input.shape
    depth = features // block
    span = rows * width

    def blocks(part):
        return part.reshape(block, depth, span)

    def matrices(received, tall):
        grid = received.reshape(tall, cols, depth, rows, width)
        return grid.transpose(2, 0, 3, 1, 4).reshape(depth, tall * rows, cols * width)

    def pieces(mixture, tall):
        grid = mixture.reshape(depth, tall, rows, cols, width)
        return grid.transpose(1, 3, 0, 2, 4).reshape(tall * cols, depth, span)

    left, right, gating = project_in(pair_input, first_gain, first_project, first_gate)
    left, right = exchange(
        ((False, False), (False, True)), sizes, 0, blocks(left), blocks(right)
    )
    mixture = jnp.einsum(
        "cik,cjk->cij",
        matrices(left, inner),
        matrices(right, halves * inner),
        preferred_element_type=jnp.float32,
    ).astype(jnp.bfloat16)
    (mixture,) = exchange(
        ((False, False),), sizes, 1, pieces(mixture, inner)
    )
    middle = finish(
        pair_input, mixture.reshape(features, span), gating, first_norm, first_final
    )
    left, right, gating = project_in(middle, second_gain, second_project, second_gate)
    left, right = exchange(
        ((False, False), (False, False)), sizes, 2, blocks(left), blocks(right)
    )
    mixture = jnp.einsum(
        "cki,ckj->cij",
        matrices(left, inner),
        matrices(right, inner),
        preferred_element_type=jnp.float32,
    ).astype(jnp.bfloat16)
    (mixture,) = exchange(
        ((True, True),), sizes, 3, pieces(mixture, halves * inner)
    )
    mixture = mixture.reshape(halves, features, span).astype(jnp.float32).sum(axis=0)
    return finish(middle, mixture, gating, second_norm, second_final)


def shards(
    pair_input,
    first_gain,
    first_project,
    first_gate,
    first_norm,
    first_final,
    second_gain,
    second_project,
    second_gate,
    second_norm,
    second_final,
):
    left_part, right_part, gating = project_in(pair_input, first_gain, first_project, first_gate)
    left_part, right_part = (
        lax.all_to_all(left_part, ("chan", "sub"), split_axis=0, concat_axis=2, tiled=True),
        lax.all_to_all(right_part, ("chan", "sub"), split_axis=0, concat_axis=2, tiled=True),
    )
    mixture = jnp.einsum(
        "cik,cjk->cij",
        left_part,
        lax.all_gather(right_part, "dap", axis=1, tiled=True),
        preferred_element_type=jnp.float32,
    ).astype(jnp.bfloat16)
    mixture = lax.all_to_all(mixture, ("chan", "sub"), split_axis=2, concat_axis=0, tiled=True)
    middle = finish(pair_input, mixture, gating, first_norm, first_final)
    left_part, right_part, gating = project_in(middle, second_gain, second_project, second_gate)
    left_part, right_part = (
        lax.all_to_all(left_part, ("chan", "sub"), split_axis=0, concat_axis=2, tiled=True),
        lax.all_to_all(right_part, ("chan", "sub"), split_axis=0, concat_axis=2, tiled=True),
    )
    turned = lax.all_to_all(left_part, "dap", split_axis=2, concat_axis=1, tiled=True)
    mixture = jnp.einsum(
        "cki,ckj->cij",
        turned,
        lax.all_gather(right_part, "dap", axis=1, tiled=True),
        preferred_element_type=jnp.float32,
    )
    mixture = lax.all_to_all(
        mixture.astype(jnp.bfloat16), ("chan", "sub"), split_axis=2, concat_axis=0, tiled=True
    )
    return finish(middle, mixture, gating, second_norm, second_final)


def solution(mesh):
    placed = (
        P(("groups", "dap"), ("chan", "sub"), None),
        P(),
        P(),
        P(),
        P(),
        P(),
        P(),
        P(),
        P(),
        P(),
        P(),
    )
    chans, subs, rows = mesh.shape["chan"], mesh.shape["sub"], mesh.shape["dap"]
    halves = 2 if rows % 2 == 0 else 1
    sizes = (halves, rows // halves, chans, subs)
    direct = functools.partial(direct_shards, sizes)

    def chosen(pair_input, *weights):
        features = pair_input.shape[2]
        if features % (16 * (rows // halves) * chans * subs) == 0:
            return direct(pair_input, *weights)
        return shards(pair_input, *weights)

    return jax.shard_map(
        chosen,
        mesh=mesh,
        in_specs=placed,
        out_specs=P(("groups", "dap"), ("chan", "sub"), None),
        check_vma=False,
    )
```

```python
import functools

import jax
import jax.numpy as jnp
from jax import lax
from jax.experimental import pallas as pl
from jax.experimental.pallas import tpu as pltpu
from jax.sharding import PartitionSpec as P

epsilon = 1e-05


def layer_norm(values, norm_gain, reduce_axis):
    average = jnp.mean(values, axis=reduce_axis, keepdims=True)
    centred = values - average
    variance = jnp.mean(centred * centred, axis=reduce_axis, keepdims=True)
    return centred * lax.rsqrt(variance + epsilon) * norm_gain


def project_in(pair_state, norm_gain, project, gate_matrix):
    row_count, col_count, features = pair_state.shape
    flattened = pair_state.reshape(row_count * col_count, features).astype(jnp.float32)
    normed = layer_norm(flattened, norm_gain, 1).astype(jnp.bfloat16)
    projected = jnp.einsum("xc,cd->dx", normed, project, preferred_element_type=jnp.float32)
    left_part = jax.nn.sigmoid(projected[:features]) * projected[features : 2 * features]
    right_part = jax.nn.sigmoid(projected[2 * features : 3 * features]) * projected[3 * features :]
    left_part = left_part.astype(jnp.bfloat16).reshape(features, row_count, col_count)
    right_part = right_part.astype(jnp.bfloat16).reshape(features, row_count, col_count)
    gating = jax.nn.sigmoid(jnp.dot(normed, gate_matrix, preferred_element_type=jnp.float32))
    return (left_part, right_part, gating)


def finish(pair_state, mixture, gating, out_gain, final_matrix):
    features = mixture.shape[0]
    flattened = mixture.reshape(features, -1).astype(jnp.float32)
    normed = layer_norm(flattened, out_gain[:, None], 0).astype(jnp.bfloat16)
    update = jnp.einsum("cx,cd->xd", normed, final_matrix, preferred_element_type=jnp.float32)
    result = pair_state.reshape(-1, features).astype(jnp.float32) + gating * update
    return result.astype(jnp.bfloat16).reshape(pair_state.shape)


def exchange_kernel(plan, sizes, *refs):
    halves, inner, chans, subs = sizes
    cols = chans * subs
    block = inner * cols
    count = len(plan)
    sources, targets = refs[:count], refs[count : 2 * count]
    sems = refs[2 * count : 5 * count]
    row = lax.axis_index("dap")
    col = lax.axis_index("chan") * subs + lax.axis_index("sub")
    mine = lax.rem(row, inner) * cols + col
    half = row // inner
    whole = halves * block
    me = row * cols + col

    def place(q):
        owner_row, owner_col = q // cols, lax.rem(q, cols)
        return {"dap": owner_row, "chan": owner_col // subs, "sub": lax.rem(owner_col, subs)}

    barrier = pltpu.get_barrier_semaphore()
    everyone = any(spans for _, spans in plan)
    reach = whole if everyone else block
    for off in range(1, reach):
        q = lax.rem(me + off, whole) if everyone else half * block + lax.rem(mine + off, block)
        pl.semaphore_signal(barrier, inc=1, device_id=place(q), device_id_type=pl.DeviceIdType.MESH)
    pl.semaphore_wait(barrier, reach - 1)

    started = []
    for off in range(0, reach):
        for (varies, spans), source, target, (sent, got, kept) in zip(
            plan, sources, targets, [sems[3 * n : 3 * n + 3] for n in range(count)]
        ):
            if spans:
                q = lax.rem(me + off, whole)
                slot, back = me, lax.rem(me - off + whole, whole)
            elif off < block:
                q = half * block + lax.rem(mine + off, block)
                slot, back = mine, lax.rem(mine - off + block, block)
            else:
                continue
            piece = source.at[q if varies else lax.rem(q, block)]
            if off == 0:
                copy = pltpu.make_async_copy(piece, target.at[slot], kept)
                copy.start()
                started.append((copy, None))
                continue
            copy = pltpu.make_async_remote_copy(
                src_ref=piece,
                dst_ref=target.at[slot],
                send_sem=sent.at[off],
                recv_sem=got.at[off],
                device_id=place(q),
                device_id_type=pl.DeviceIdType.MESH,
            )
            copy.start()
            arriving = pltpu.make_async_remote_copy(
                src_ref=piece,
                dst_ref=target.at[back],
                send_sem=sent.at[off],
                recv_sem=got.at[off],
                device_id=place(q),
                device_id_type=pl.DeviceIdType.MESH,
            )
            started.append((copy, arriving))
    for copy, arriving in started:
        if arriving is None:
            copy.wait()
        else:
            copy.wait_send()
            arriving.wait_recv()


def exchange(plan, sizes, number, *arrays):
    halves, inner, chans, subs = sizes
    block = inner * chans * subs
    shapes, sems = [], []
    for (varies, spans), array in zip(plan, arrays):
        slots = halves * block if spans else block
        shapes.append(jax.ShapeDtypeStruct((slots,) + array.shape[1:], array.dtype))
        sems += [
            pltpu.SemaphoreType.DMA((slots,)),
            pltpu.SemaphoreType.DMA((slots,)),
            pltpu.SemaphoreType.DMA,
        ]
    return pl.pallas_call(
        functools.partial(exchange_kernel, plan, sizes),
        out_shape=shapes,
        in_specs=[pl.BlockSpec(memory_space=pl.ANY)] * len(arrays),
        out_specs=[pl.BlockSpec(memory_space=pl.ANY)] * len(arrays),
        scratch_shapes=sems,
        compiler_params=pltpu.CompilerParams(collective_id=number, has_side_effects=True),
    )(*arrays)


def product_kernel(turned, left_ref, right_ref, out_ref):
    left_tall, cols, depth, rows, width = left_ref.shape
    right_tall = right_ref.shape[0]

    def matrix(ref, tall, channel):
        return jnp.concatenate(
            [
                jnp.concatenate([ref[t, x, channel] for x in range(cols)], axis=1)
                for t in range(tall)
            ],
            axis=0,
        )

    side = 0 if turned else 1
    for channel in range(depth):
        mixed = lax.dot_general(
            matrix(left_ref, left_tall, channel),
            matrix(right_ref, right_tall, channel),
            (((side,), (side,)), ((), ())),
            preferred_element_type=jnp.float32,
        ).astype(out_ref.dtype)
        for t in range(out_ref.shape[0]):
            for x in range(cols):
                out_ref[t, x, channel] = mixed[
                    t * rows : (t + 1) * rows, x * width : (x + 1) * width
                ]


def product(turned, left, right):
    left_tall, cols, depth, rows, width = left.shape
    right_tall = right.shape[0]
    tall = cols if turned else left_tall
    step = 4 if depth % 4 == 0 else 1

    def spec(high):
        return pl.BlockSpec((high, cols, step, rows, width), lambda n: (0, 0, n, 0, 0))

    flops = 2 * depth * (tall * rows) * (cols * width) * (left_tall * rows if turned else cols * width)
    return pl.pallas_call(
        functools.partial(product_kernel, turned),
        out_shape=jax.ShapeDtypeStruct((tall, cols, depth, rows, width), jnp.bfloat16),
        grid=(depth // step,),
        in_specs=[spec(left_tall), spec(right_tall)],
        out_specs=spec(tall),
        compiler_params=pltpu.CompilerParams(vmem_limit_bytes=40 * 2**20),
        cost_estimate=pl.CostEstimate(
            flops=flops, bytes_accessed=2 * (left.size + right.size), transcendentals=0
        ),
    )(left, right)


def direct_shards(
    sizes,
    pair_input,
    first_gain,
    first_project,
    first_gate,
    first_norm,
    first_final,
    second_gain,
    second_project,
    second_gate,
    second_norm,
    second_final,
):
    halves, inner, chans, subs = sizes
    cols = chans * subs
    block = inner * cols
    rows, width, features = pair_input.shape
    depth = features // block
    span = rows * width

    def blocks(part):
        return part.reshape(-1, depth, span)

    def grid(received, tall):
        return received.reshape(tall, cols, depth, rows, width)

    left, right, gating = project_in(pair_input, first_gain, first_project, first_gate)
    left, right = exchange(
        ((False, False), (False, True)), sizes, 0, blocks(left), blocks(right)
    )
    mixture = product(False, grid(left, inner), grid(right, halves * inner))
    (mixture,) = exchange(((False, False),), sizes, 1, blocks(mixture))
    middle = finish(
        pair_input, mixture.reshape(features, span), gating, first_norm, first_final
    )
    left, right, gating = project_in(middle, second_gain, second_project, second_gate)
    left, right = exchange(
        ((False, False), (False, False)), sizes, 2, blocks(left), blocks(right)
    )
    mixture = product(True, grid(left, inner), grid(right, inner))
    (mixture,) = exchange(((True, True),), sizes, 3, blocks(mixture))
    mixture = mixture.reshape(halves, features, span).astype(jnp.float32).sum(axis=0)
    return finish(middle, mixture, gating, second_norm, second_final)


def shards(
    pair_input,
    first_gain,
    first_project,
    first_gate,
    first_norm,
    first_final,
    second_gain,
    second_project,
    second_gate,
    second_norm,
    second_final,
):
    left_part, right_part, gating = project_in(pair_input, first_gain, first_project, first_gate)
    left_part, right_part = (
        lax.all_to_all(left_part, ("chan", "sub"), split_axis=0, concat_axis=2, tiled=True),
        lax.all_to_all(right_part, ("chan", "sub"), split_axis=0, concat_axis=2, tiled=True),
    )
    mixture = jnp.einsum(
        "cik,cjk->cij",
        left_part,
        lax.all_gather(right_part, "dap", axis=1, tiled=True),
        preferred_element_type=jnp.float32,
    ).astype(jnp.bfloat16)
    mixture = lax.all_to_all(mixture, ("chan", "sub"), split_axis=2, concat_axis=0, tiled=True)
    middle = finish(pair_input, mixture, gating, first_norm, first_final)
    left_part, right_part, gating = project_in(middle, second_gain, second_project, second_gate)
    left_part, right_part = (
        lax.all_to_all(left_part, ("chan", "sub"), split_axis=0, concat_axis=2, tiled=True),
        lax.all_to_all(right_part, ("chan", "sub"), split_axis=0, concat_axis=2, tiled=True),
    )
    turned = lax.all_to_all(left_part, "dap", split_axis=2, concat_axis=1, tiled=True)
    mixture = jnp.einsum(
        "cki,ckj->cij",
        turned,
        lax.all_gather(right_part, "dap", axis=1, tiled=True),
        preferred_element_type=jnp.float32,
    )
    mixture = lax.all_to_all(
        mixture.astype(jnp.bfloat16), ("chan", "sub"), split_axis=2, concat_axis=0, tiled=True
    )
    return finish(middle, mixture, gating, second_norm, second_final)


def solution(mesh):
    placed = (
        P(("groups", "dap"), ("chan", "sub"), None),
        P(),
        P(),
        P(),
        P(),
        P(),
        P(),
        P(),
        P(),
        P(),
        P(),
    )
    chans, subs, rows = mesh.shape["chan"], mesh.shape["sub"], mesh.shape["dap"]
    halves = 2 if rows % 2 == 0 else 1
    sizes = (halves, rows // halves, chans, subs)
    direct = functools.partial(direct_shards, sizes)

    def chosen(pair_input, *weights):
        features = pair_input.shape[2]
        square = pair_input.shape[0] == pair_input.shape[1] and rows == chans * subs
        if square and features % (16 * (rows // halves) * chans * subs) == 0:
            return direct(pair_input, *weights)
        return shards(pair_input, *weights)

    return jax.shard_map(
        chosen,
        mesh=mesh,
        in_specs=placed,
        out_specs=P(("groups", "dap"), ("chan", "sub"), None),
        check_vma=False,
    )
```

```python
import functools

import jax
import jax.numpy as jnp
from jax import lax
from jax.experimental import pallas as pl
from jax.experimental.pallas import tpu as pltpu
from jax.sharding import PartitionSpec as P

epsilon = 1e-05


def layer_norm(values, norm_gain, reduce_axis):
    average = jnp.mean(values, axis=reduce_axis, keepdims=True)
    centred = values - average
    variance = jnp.mean(centred * centred, axis=reduce_axis, keepdims=True)
    return centred * lax.rsqrt(variance + epsilon) * norm_gain


def project_in(pair_state, norm_gain, project, gate_matrix):
    row_count, col_count, features = pair_state.shape
    flattened = pair_state.reshape(row_count * col_count, features).astype(jnp.float32)
    normed = layer_norm(flattened, norm_gain, 1).astype(jnp.bfloat16)
    projected = jnp.einsum("xc,cd->dx", normed, project, preferred_element_type=jnp.float32)
    left_part = jax.nn.sigmoid(projected[:features]) * projected[features : 2 * features]
    right_part = jax.nn.sigmoid(projected[2 * features : 3 * features]) * projected[3 * features :]
    left_part = left_part.astype(jnp.bfloat16).reshape(features, row_count, col_count)
    right_part = right_part.astype(jnp.bfloat16).reshape(features, row_count, col_count)
    gating = jax.nn.sigmoid(jnp.dot(normed, gate_matrix, preferred_element_type=jnp.float32))
    return (left_part, right_part, gating)


def finish(pair_state, mixture, gating, out_gain, final_matrix):
    features = mixture.shape[0]
    flattened = mixture.reshape(features, -1).astype(jnp.float32)
    normed = layer_norm(flattened, out_gain[:, None], 0).astype(jnp.bfloat16)
    update = jnp.einsum("cx,cd->xd", normed, final_matrix, preferred_element_type=jnp.float32)
    result = pair_state.reshape(-1, features).astype(jnp.float32) + gating * update
    return result.astype(jnp.bfloat16).reshape(pair_state.shape)


def exchange_kernel(plan, sizes, opened, *refs):
    halves, inner, chans, subs = sizes
    cols = chans * subs
    block = inner * cols
    count = len(plan)
    sources, targets = refs[:count], refs[count : 2 * count]
    sems = refs[2 * count : 5 * count]
    opens = targets
    if opened:
        targets = refs[5 * count : 6 * count]
    row = lax.axis_index("dap")
    col = lax.axis_index("chan") * subs + lax.axis_index("sub")
    mine = lax.rem(row, inner) * cols + col
    half = row // inner
    whole = halves * block
    me = row * cols + col

    def place(q):
        owner_row, owner_col = q // cols, lax.rem(q, cols)
        return {"dap": owner_row, "chan": owner_col // subs, "sub": lax.rem(owner_col, subs)}

    barrier = pltpu.get_barrier_semaphore()
    everyone = any(spans for _, spans in plan)
    reach = whole if everyone else block
    for off in range(1, reach):
        q = lax.rem(me + off, whole) if everyone else half * block + lax.rem(mine + off, block)
        pl.semaphore_signal(barrier, inc=1, device_id=place(q), device_id_type=pl.DeviceIdType.MESH)
    pl.semaphore_wait(barrier, reach - 1)

    started = []
    for off in range(0, reach):
        for (varies, spans), source, target, (sent, got, kept) in zip(
            plan, sources, targets, [sems[3 * n : 3 * n + 3] for n in range(count)]
        ):
            if spans:
                q = lax.rem(me + off, whole)
                slot, back = me, lax.rem(me - off + whole, whole)
            elif off < block:
                q = half * block + lax.rem(mine + off, block)
                slot, back = mine, lax.rem(mine - off + block, block)
            else:
                continue
            piece = source.at[q if varies else lax.rem(q, block)]
            if off == 0:
                copy = pltpu.make_async_copy(piece, target.at[slot], kept)
                copy.start()
                started.append((copy, None))
                continue
            copy = pltpu.make_async_remote_copy(
                src_ref=piece,
                dst_ref=target.at[slot],
                send_sem=sent.at[off],
                recv_sem=got.at[off],
                device_id=place(q),
                device_id_type=pl.DeviceIdType.MESH,
            )
            copy.start()
            if opened:
                started.append((copy, copy))
                continue
            arriving = pltpu.make_async_remote_copy(
                src_ref=piece,
                dst_ref=target.at[back],
                send_sem=sent.at[off],
                recv_sem=got.at[off],
                device_id=place(q),
                device_id_type=pl.DeviceIdType.MESH,
            )
            started.append((copy, arriving))
    if not opened:
        for copy, arriving in started:
            if arriving is None:
                copy.wait()
            else:
                copy.wait_send()
                arriving.wait_recv()
        return

    def unfold(target, open_ref, slot):
        rows, width = open_ref.shape[2:]
        open_ref[slot] = target[slot].reshape(target.shape[1], rows, width)

    for (varies, spans), source, target, open_ref, (sent, got, kept) in zip(
        plan, sources, targets, opens, [sems[3 * n : 3 * n + 3] for n in range(count)]
    ):
        slots = whole if spans else block
        base = me if spans else mine
        pltpu.make_async_copy(source.at[me if varies else mine], target.at[base], kept).wait()
        unfold(target, open_ref, base)

        def arrive(off, carry, slots=slots, base=base, source=source, target=target,
                   open_ref=open_ref, sent=sent, got=got):
            back = lax.rem(base - off + slots, slots)
            arriving = pltpu.make_async_remote_copy(
                src_ref=source.at[0],
                dst_ref=target.at[back],
                send_sem=sent.at[off],
                recv_sem=got.at[off],
                device_id=place(back if slots == whole else half * block + back),
                device_id_type=pl.DeviceIdType.MESH,
            )
            arriving.wait_recv()
            unfold(target, open_ref, back)
            return carry

        lax.fori_loop(1, slots, arrive, 0)
    for copy, arriving in started:
        if arriving is not None:
            copy.wait_send()


def exchange(plan, sizes, number, *arrays, opened=None):
    halves, inner, chans, subs = sizes
    block = inner * chans * subs
    shapes, sems, landing = [], [], []
    for (varies, spans), array in zip(plan, arrays):
        slots = halves * block if spans else block
        if opened:
            shapes.append(jax.ShapeDtypeStruct((slots, array.shape[1]) + opened, array.dtype))
            landing.append(pltpu.VMEM((slots,) + array.shape[1:], array.dtype))
        else:
            shapes.append(jax.ShapeDtypeStruct((slots,) + array.shape[1:], array.dtype))
        sems += [
            pltpu.SemaphoreType.DMA((slots,)),
            pltpu.SemaphoreType.DMA((slots,)),
            pltpu.SemaphoreType.DMA,
        ]
    return pl.pallas_call(
        functools.partial(exchange_kernel, plan, sizes, opened is not None),
        out_shape=shapes,
        in_specs=[pl.BlockSpec(memory_space=pl.ANY)] * len(arrays),
        out_specs=[pl.BlockSpec(memory_space=pltpu.VMEM if opened else pl.ANY)] * len(arrays),
        scratch_shapes=sems + landing,
        compiler_params=pltpu.CompilerParams(
            collective_id=number,
            has_side_effects=True,
            vmem_limit_bytes=40 * 2**20 if opened else None,
        ),
    )(*arrays)


def product_kernel(turned, left_ref, right_ref, out_ref):
    left_tall, cols, depth, rows, width = left_ref.shape
    right_tall = right_ref.shape[0]

    def matrix(ref, tall, channel):
        return jnp.concatenate(
            [
                jnp.concatenate([ref[t, x, channel] for x in range(cols)], axis=1)
                for t in range(tall)
            ],
            axis=0,
        )

    side = 0 if turned else 1
    for channel in range(depth):
        mixed = lax.dot_general(
            matrix(left_ref, left_tall, channel),
            matrix(right_ref, right_tall, channel),
            (((side,), (side,)), ((), ())),
            preferred_element_type=jnp.float32,
        ).astype(out_ref.dtype)
        for t in range(out_ref.shape[0]):
            for x in range(cols):
                out_ref[t, x, channel] = mixed[
                    t * rows : (t + 1) * rows, x * width : (x + 1) * width
                ]


def product(turned, left, right):
    left_tall, cols, depth, rows, width = left.shape
    right_tall = right.shape[0]
    tall = cols if turned else left_tall
    step = 4 if depth % 4 == 0 else 1

    def spec(high):
        return pl.BlockSpec((high, cols, step, rows, width), lambda n: (0, 0, n, 0, 0))

    flops = 2 * depth * (tall * rows) * (cols * width) * (left_tall * rows if turned else cols * width)
    return pl.pallas_call(
        functools.partial(product_kernel, turned),
        out_shape=jax.ShapeDtypeStruct((tall, cols, depth, rows, width), jnp.bfloat16),
        grid=(depth // step,),
        in_specs=[spec(left_tall), spec(right_tall)],
        out_specs=spec(tall),
        compiler_params=pltpu.CompilerParams(vmem_limit_bytes=40 * 2**20),
        cost_estimate=pl.CostEstimate(
            flops=flops, bytes_accessed=2 * (left.size + right.size), transcendentals=0
        ),
    )(left, right)


def direct_shards(
    sizes,
    pair_input,
    first_gain,
    first_project,
    first_gate,
    first_norm,
    first_final,
    second_gain,
    second_project,
    second_gate,
    second_norm,
    second_final,
):
    halves, inner, chans, subs = sizes
    cols = chans * subs
    block = inner * cols
    rows, width, features = pair_input.shape
    depth = features // block
    span = rows * width

    def blocks(part):
        return part.reshape(-1, depth, span)

    def grid(received, tall):
        return received.reshape(tall, cols, depth, rows, width)

    left, right, gating = project_in(pair_input, first_gain, first_project, first_gate)
    left, right = exchange(
        ((False, False), (False, True)), sizes, 0, blocks(left), blocks(right),
        opened=(rows, width),
    )
    mixture = product(False, grid(left, inner), grid(right, halves * inner))
    (mixture,) = exchange(((False, False),), sizes, 1, blocks(mixture))
    middle = finish(
        pair_input, mixture.reshape(features, span), gating, first_norm, first_final
    )
    left, right, gating = project_in(middle, second_gain, second_project, second_gate)
    left, right = exchange(
        ((False, False), (False, False)), sizes, 2, blocks(left), blocks(right),
        opened=(rows, width),
    )
    mixture = product(True, grid(left, inner), grid(right, inner))
    (mixture,) = exchange(((True, True),), sizes, 3, blocks(mixture))
    mixture = mixture.reshape(halves, features, span)
    mixture = sum(mixture[n].astype(jnp.float32) for n in range(halves))
    return finish(middle, mixture, gating, second_norm, second_final)


def shards(
    pair_input,
    first_gain,
    first_project,
    first_gate,
    first_norm,
    first_final,
    second_gain,
    second_project,
    second_gate,
    second_norm,
    second_final,
):
    left_part, right_part, gating = project_in(pair_input, first_gain, first_project, first_gate)
    left_part, right_part = (
        lax.all_to_all(left_part, ("chan", "sub"), split_axis=0, concat_axis=2, tiled=True),
        lax.all_to_all(right_part, ("chan", "sub"), split_axis=0, concat_axis=2, tiled=True),
    )
    mixture = jnp.einsum(
        "cik,cjk->cij",
        left_part,
        lax.all_gather(right_part, "dap", axis=1, tiled=True),
        preferred_element_type=jnp.float32,
    ).astype(jnp.bfloat16)
    mixture = lax.all_to_all(mixture, ("chan", "sub"), split_axis=2, concat_axis=0, tiled=True)
    middle = finish(pair_input, mixture, gating, first_norm, first_final)
    left_part, right_part, gating = project_in(middle, second_gain, second_project, second_gate)
    left_part, right_part = (
        lax.all_to_all(left_part, ("chan", "sub"), split_axis=0, concat_axis=2, tiled=True),
        lax.all_to_all(right_part, ("chan", "sub"), split_axis=0, concat_axis=2, tiled=True),
    )
    turned = lax.all_to_all(left_part, "dap", split_axis=2, concat_axis=1, tiled=True)
    mixture = jnp.einsum(
        "cki,ckj->cij",
        turned,
        lax.all_gather(right_part, "dap", axis=1, tiled=True),
        preferred_element_type=jnp.float32,
    )
    mixture = lax.all_to_all(
        mixture.astype(jnp.bfloat16), ("chan", "sub"), split_axis=2, concat_axis=0, tiled=True
    )
    return finish(middle, mixture, gating, second_norm, second_final)


def solution(mesh):
    placed = (
        P(("groups", "dap"), ("chan", "sub"), None),
        P(),
        P(),
        P(),
        P(),
        P(),
        P(),
        P(),
        P(),
        P(),
        P(),
    )
    chans, subs, rows = mesh.shape["chan"], mesh.shape["sub"], mesh.shape["dap"]
    halves = 2 if rows % 2 == 0 else 1
    sizes = (halves, rows // halves, chans, subs)
    direct = functools.partial(direct_shards, sizes)

    def chosen(pair_input, *weights):
        features = pair_input.shape[2]
        square = pair_input.shape[0] == pair_input.shape[1] and rows == chans * subs
        if square and features % (16 * (rows // halves) * chans * subs) == 0:
            return direct(pair_input, *weights)
        return shards(pair_input, *weights)

    return jax.shard_map(
        chosen,
        mesh=mesh,
        in_specs=placed,
        out_specs=P(("groups", "dap"), ("chan", "sub"), None),
        check_vma=False,
    )
```

```python
import functools

import jax
import jax.numpy as jnp
from jax import lax
from jax.experimental import pallas as pl
from jax.experimental.pallas import tpu as pltpu
from jax.sharding import PartitionSpec as P

epsilon = 1e-05


def layer_norm(values, norm_gain, reduce_axis):
    average = jnp.mean(values, axis=reduce_axis, keepdims=True)
    centred = values - average
    variance = jnp.mean(centred * centred, axis=reduce_axis, keepdims=True)
    return centred * lax.rsqrt(variance + epsilon) * norm_gain


def project_in(pair_state, norm_gain, project, gate_matrix):
    row_count, col_count, features = pair_state.shape
    flattened = pair_state.reshape(row_count * col_count, features).astype(jnp.float32)
    normed = layer_norm(flattened, norm_gain, 1).astype(jnp.bfloat16)
    projected = jnp.einsum("xc,cd->dx", normed, project, preferred_element_type=jnp.float32)
    left_part = jax.nn.sigmoid(projected[:features]) * projected[features : 2 * features]
    right_part = jax.nn.sigmoid(projected[2 * features : 3 * features]) * projected[3 * features :]
    left_part = left_part.astype(jnp.bfloat16).reshape(features, row_count, col_count)
    right_part = right_part.astype(jnp.bfloat16).reshape(features, row_count, col_count)
    gating = jax.nn.sigmoid(jnp.dot(normed, gate_matrix, preferred_element_type=jnp.float32))
    return (left_part, right_part, gating)


def finish(pair_state, mixture, gating, out_gain, final_matrix):
    features = mixture.shape[0]
    flattened = mixture.reshape(features, -1).astype(jnp.float32)
    normed = layer_norm(flattened, out_gain[:, None], 0).astype(jnp.bfloat16)
    update = jnp.einsum("cx,cd->xd", normed, final_matrix, preferred_element_type=jnp.float32)
    result = pair_state.reshape(-1, features).astype(jnp.float32) + gating * update
    return result.astype(jnp.bfloat16).reshape(pair_state.shape)


def exchange_kernel(plan, sizes, opened, *refs):
    halves, inner, chans, subs = sizes
    cols = chans * subs
    block = inner * cols
    count = len(plan)
    sources, targets = refs[:count], refs[count : 2 * count]
    sems = refs[2 * count : 5 * count]
    opens = targets
    if opened:
        targets = refs[5 * count : 6 * count]
    row = lax.axis_index("dap")
    col = lax.axis_index("chan") * subs + lax.axis_index("sub")
    mine = lax.rem(row, inner) * cols + col
    half = row // inner
    whole = halves * block
    me = row * cols + col

    def place(q):
        owner_row, owner_col = q // cols, lax.rem(q, cols)
        return {"dap": owner_row, "chan": owner_col // subs, "sub": lax.rem(owner_col, subs)}

    barrier = pltpu.get_barrier_semaphore()
    everyone = any(spans for _, spans in plan)
    reach = whole if everyone else block
    for off in range(1, reach):
        q = lax.rem(me + off, whole) if everyone else half * block + lax.rem(mine + off, block)
        pl.semaphore_signal(barrier, inc=1, device_id=place(q), device_id_type=pl.DeviceIdType.MESH)
    pl.semaphore_wait(barrier, reach - 1)

    started = []
    for off in range(0, reach):
        for (varies, spans), source, target, (sent, got, kept) in zip(
            plan, sources, targets, [sems[3 * n : 3 * n + 3] for n in range(count)]
        ):
            if spans:
                q = lax.rem(me + off, whole)
                slot, back = me, lax.rem(me - off + whole, whole)
            elif off < block:
                q = half * block + lax.rem(mine + off, block)
                slot, back = mine, lax.rem(mine - off + block, block)
            else:
                continue
            piece = source.at[q if varies else lax.rem(q, block)]
            if off == 0:
                copy = pltpu.make_async_copy(piece, target.at[slot], kept)
                copy.start()
                started.append((copy, None))
                continue
            copy = pltpu.make_async_remote_copy(
                src_ref=piece,
                dst_ref=target.at[slot],
                send_sem=sent.at[off],
                recv_sem=got.at[off],
                device_id=place(q),
                device_id_type=pl.DeviceIdType.MESH,
            )
            copy.start()
            if opened:
                started.append((copy, copy))
                continue
            arriving = pltpu.make_async_remote_copy(
                src_ref=piece,
                dst_ref=target.at[back],
                send_sem=sent.at[off],
                recv_sem=got.at[off],
                device_id=place(q),
                device_id_type=pl.DeviceIdType.MESH,
            )
            started.append((copy, arriving))
    if not opened:
        for copy, arriving in started:
            if arriving is None:
                copy.wait()
            else:
                copy.wait_send()
                arriving.wait_recv()
        return

    def unfold(target, open_ref, slot):
        rows, width = open_ref.shape[2:]
        open_ref[slot] = target[slot].reshape(target.shape[1], rows, width)

    for (varies, spans), source, target, open_ref, (sent, got, kept) in zip(
        plan, sources, targets, opens, [sems[3 * n : 3 * n + 3] for n in range(count)]
    ):
        slots = whole if spans else block
        base = me if spans else mine
        pltpu.make_async_copy(source.at[me if varies else mine], target.at[base], kept).wait()
        unfold(target, open_ref, base)

        def arrive(off, carry, slots=slots, base=base, source=source, target=target,
                   open_ref=open_ref, sent=sent, got=got):
            back = lax.rem(base - off + slots, slots)
            arriving = pltpu.make_async_remote_copy(
                src_ref=source.at[0],
                dst_ref=target.at[back],
                send_sem=sent.at[off],
                recv_sem=got.at[off],
                device_id=place(back if slots == whole else half * block + back),
                device_id_type=pl.DeviceIdType.MESH,
            )
            arriving.wait_recv()
            unfold(target, open_ref, back)
            return carry

        lax.fori_loop(1, slots, arrive, 0)
    for copy, arriving in started:
        if arriving is not None:
            copy.wait_send()


def fold_kernel(spans, sizes, source, target, sent, got, kept, flat):
    halves, inner, chans, subs = sizes
    cols = chans * subs
    block = inner * cols
    slots = halves * block if spans else block
    row = lax.axis_index("dap")
    col = lax.axis_index("chan") * subs + lax.axis_index("sub")
    first = 0 if spans else (row // inner) * block
    base = row * cols + col - first

    def place(q):
        owner_row, owner_col = (first + q) // cols, lax.rem(q, cols)
        return {"dap": owner_row, "chan": owner_col // subs, "sub": lax.rem(owner_col, subs)}

    def push(off, slot):
        q = lax.rem(base + off, slots)
        return pltpu.make_async_remote_copy(
            src_ref=flat.at[q],
            dst_ref=target.at[slot],
            send_sem=sent.at[off],
            recv_sem=got.at[off],
            device_id=place(q),
            device_id_type=pl.DeviceIdType.MESH,
        )

    def fold(q):
        flat[q] = source[q].reshape(flat.shape[1:])

    barrier = pltpu.get_barrier_semaphore()
    for off in range(1, slots):
        pl.semaphore_signal(
            barrier,
            inc=1,
            device_id=place(lax.rem(base + off, slots)),
            device_id_type=pl.DeviceIdType.MESH,
        )
    pl.semaphore_wait(barrier, slots - 1)

    def send(off, carry):
        fold(lax.rem(base + off, slots))
        push(off, base).start()
        return carry

    lax.fori_loop(1, slots, send, 0)
    fold(base)
    own = pltpu.make_async_copy(flat.at[base], target.at[base], kept)
    own.start()

    def finish_off(off, carry):
        copy = push(off, lax.rem(base - off + slots, slots))
        copy.wait_send()
        copy.wait_recv()
        return carry

    lax.fori_loop(1, slots, finish_off, 0)
    own.wait()


def fold_exchange(spans, sizes, number, array):
    slots, depth, rows, width = array.shape
    flat = (slots, depth, rows * width)
    return pl.pallas_call(
        functools.partial(fold_kernel, spans, sizes),
        out_shape=jax.ShapeDtypeStruct(flat, array.dtype),
        in_specs=[pl.BlockSpec(memory_space=pltpu.VMEM)],
        out_specs=pl.BlockSpec(memory_space=pl.ANY),
        scratch_shapes=[
            pltpu.SemaphoreType.DMA((slots,)),
            pltpu.SemaphoreType.DMA((slots,)),
            pltpu.SemaphoreType.DMA,
            pltpu.VMEM(flat, array.dtype),
        ],
        compiler_params=pltpu.CompilerParams(
            collective_id=number, has_side_effects=True, vmem_limit_bytes=24 * 2**20
        ),
    )(array)


def exchange(plan, sizes, number, *arrays, opened=None):
    halves, inner, chans, subs = sizes
    block = inner * chans * subs
    shapes, sems, landing = [], [], []
    for (varies, spans), array in zip(plan, arrays):
        slots = halves * block if spans else block
        if opened:
            shapes.append(jax.ShapeDtypeStruct((slots, array.shape[1]) + opened, array.dtype))
            landing.append(pltpu.VMEM((slots,) + array.shape[1:], array.dtype))
        else:
            shapes.append(jax.ShapeDtypeStruct((slots,) + array.shape[1:], array.dtype))
        sems += [
            pltpu.SemaphoreType.DMA((slots,)),
            pltpu.SemaphoreType.DMA((slots,)),
            pltpu.SemaphoreType.DMA,
        ]
    return pl.pallas_call(
        functools.partial(exchange_kernel, plan, sizes, opened is not None),
        out_shape=shapes,
        in_specs=[pl.BlockSpec(memory_space=pl.ANY)] * len(arrays),
        out_specs=[pl.BlockSpec(memory_space=pltpu.VMEM if opened else pl.ANY)] * len(arrays),
        scratch_shapes=sems + landing,
        compiler_params=pltpu.CompilerParams(
            collective_id=number,
            has_side_effects=True,
            vmem_limit_bytes=24 * 2**20 if opened else None,
        ),
    )(*arrays)


def product_kernel(turned, left_ref, right_ref, out_ref):
    left_tall, cols, depth, rows, width = left_ref.shape
    right_tall = right_ref.shape[0]

    def matrix(ref, tall, channel):
        return jnp.concatenate(
            [
                jnp.concatenate([ref[t, x, channel] for x in range(cols)], axis=1)
                for t in range(tall)
            ],
            axis=0,
        )

    side = 0 if turned else 1
    for channel in range(depth):
        mixed = lax.dot_general(
            matrix(left_ref, left_tall, channel),
            matrix(right_ref, right_tall, channel),
            (((side,), (side,)), ((), ())),
            preferred_element_type=jnp.float32,
        ).astype(out_ref.dtype)
        for t in range(out_ref.shape[0]):
            for x in range(cols):
                out_ref[t, x, channel] = mixed[
                    t * rows : (t + 1) * rows, x * width : (x + 1) * width
                ]


def product(turned, left, right):
    left_tall, cols, depth, rows, width = left.shape
    right_tall = right.shape[0]
    tall = cols if turned else left_tall
    step = 4 if depth % 4 == 0 else 1

    def spec(high):
        return pl.BlockSpec((high, cols, step, rows, width), lambda n: (0, 0, n, 0, 0))

    flops = 2 * depth * (tall * rows) * (cols * width) * (left_tall * rows if turned else cols * width)
    return pl.pallas_call(
        functools.partial(product_kernel, turned),
        out_shape=jax.ShapeDtypeStruct((tall, cols, depth, rows, width), jnp.bfloat16),
        grid=(depth // step,),
        in_specs=[spec(left_tall), spec(right_tall)],
        out_specs=spec(tall),
        compiler_params=pltpu.CompilerParams(vmem_limit_bytes=24 * 2**20),
        cost_estimate=pl.CostEstimate(
            flops=flops, bytes_accessed=2 * (left.size + right.size), transcendentals=0
        ),
    )(left, right)


def direct_shards(
    sizes,
    pair_input,
    first_gain,
    first_project,
    first_gate,
    first_norm,
    first_final,
    second_gain,
    second_project,
    second_gate,
    second_norm,
    second_final,
):
    halves, inner, chans, subs = sizes
    cols = chans * subs
    block = inner * cols
    rows, width, features = pair_input.shape
    depth = features // block
    span = rows * width

    def blocks(part):
        return part.reshape(-1, depth, span)

    def grid(received, tall):
        return received.reshape(tall, cols, depth, rows, width)

    left, right, gating = project_in(pair_input, first_gain, first_project, first_gate)
    left, right = exchange(
        ((False, False), (False, True)), sizes, 0, blocks(left), blocks(right),
        opened=(rows, width),
    )
    mixture = product(False, grid(left, inner), grid(right, halves * inner))
    mixture = fold_exchange(False, sizes, 1, mixture.reshape(-1, depth, rows, width))
    middle = finish(
        pair_input, mixture.reshape(features, span), gating, first_norm, first_final
    )
    left, right, gating = project_in(middle, second_gain, second_project, second_gate)
    left, right = exchange(
        ((False, False), (False, False)), sizes, 2, blocks(left), blocks(right),
        opened=(rows, width),
    )
    mixture = product(True, grid(left, inner), grid(right, inner))
    mixture = fold_exchange(True, sizes, 3, mixture.reshape(-1, depth, rows, width))
    mixture = mixture.reshape(halves, features, span)
    mixture = sum(mixture[n].astype(jnp.float32) for n in range(halves))
    return finish(middle, mixture, gating, second_norm, second_final)


def shards(
    pair_input,
    first_gain,
    first_project,
    first_gate,
    first_norm,
    first_final,
    second_gain,
    second_project,
    second_gate,
    second_norm,
    second_final,
):
    left_part, right_part, gating = project_in(pair_input, first_gain, first_project, first_gate)
    left_part, right_part = (
        lax.all_to_all(left_part, ("chan", "sub"), split_axis=0, concat_axis=2, tiled=True),
        lax.all_to_all(right_part, ("chan", "sub"), split_axis=0, concat_axis=2, tiled=True),
    )
    mixture = jnp.einsum(
        "cik,cjk->cij",
        left_part,
        lax.all_gather(right_part, "dap", axis=1, tiled=True),
        preferred_element_type=jnp.float32,
    ).astype(jnp.bfloat16)
    mixture = lax.all_to_all(mixture, ("chan", "sub"), split_axis=2, concat_axis=0, tiled=True)
    middle = finish(pair_input, mixture, gating, first_norm, first_final)
    left_part, right_part, gating = project_in(middle, second_gain, second_project, second_gate)
    left_part, right_part = (
        lax.all_to_all(left_part, ("chan", "sub"), split_axis=0, concat_axis=2, tiled=True),
        lax.all_to_all(right_part, ("chan", "sub"), split_axis=0, concat_axis=2, tiled=True),
    )
    turned = lax.all_to_all(left_part, "dap", split_axis=2, concat_axis=1, tiled=True)
    mixture = jnp.einsum(
        "cki,ckj->cij",
        turned,
        lax.all_gather(right_part, "dap", axis=1, tiled=True),
        preferred_element_type=jnp.float32,
    )
    mixture = lax.all_to_all(
        mixture.astype(jnp.bfloat16), ("chan", "sub"), split_axis=2, concat_axis=0, tiled=True
    )
    return finish(middle, mixture, gating, second_norm, second_final)


def solution(mesh):
    placed = (
        P(("groups", "dap"), ("chan", "sub"), None),
        P(),
        P(),
        P(),
        P(),
        P(),
        P(),
        P(),
        P(),
        P(),
        P(),
    )
    chans, subs, rows = mesh.shape["chan"], mesh.shape["sub"], mesh.shape["dap"]
    halves = 2 if rows % 2 == 0 else 1
    sizes = (halves, rows // halves, chans, subs)
    direct = functools.partial(direct_shards, sizes)

    def chosen(pair_input, *weights):
        features = pair_input.shape[2]
        square = pair_input.shape[0] == pair_input.shape[1] and rows == chans * subs
        if square and features % (16 * (rows // halves) * chans * subs) == 0:
            return direct(pair_input, *weights)
        return shards(pair_input, *weights)

    return jax.shard_map(
        chosen,
        mesh=mesh,
        in_specs=placed,
        out_specs=P(("groups", "dap"), ("chan", "sub"), None),
        check_vma=False,
    )
```

```python
import functools

import jax
import jax.numpy as jnp
from jax import lax
from jax.experimental import pallas as pl
from jax.experimental.pallas import tpu as pltpu
from jax.sharding import PartitionSpec as P

epsilon = 1e-05


def layer_norm(values, norm_gain, reduce_axis):
    average = jnp.mean(values, axis=reduce_axis, keepdims=True)
    centred = values - average
    variance = jnp.mean(centred * centred, axis=reduce_axis, keepdims=True)
    return centred * lax.rsqrt(variance + epsilon) * norm_gain


def project_in(pair_state, norm_gain, project, gate_matrix):
    row_count, col_count, features = pair_state.shape
    flattened = pair_state.reshape(row_count * col_count, features).astype(jnp.float32)
    normed = layer_norm(flattened, norm_gain, 1).astype(jnp.bfloat16)
    projected = jnp.einsum("xc,cd->dx", normed, project, preferred_element_type=jnp.float32)
    left_part = jax.nn.sigmoid(projected[:features]) * projected[features : 2 * features]
    right_part = jax.nn.sigmoid(projected[2 * features : 3 * features]) * projected[3 * features :]
    left_part = left_part.astype(jnp.bfloat16).reshape(features, row_count, col_count)
    right_part = right_part.astype(jnp.bfloat16).reshape(features, row_count, col_count)
    gating = jax.nn.sigmoid(jnp.dot(normed, gate_matrix, preferred_element_type=jnp.float32))
    return (left_part, right_part, gating)


def finish(pair_state, mixture, gating, out_gain, final_matrix):
    features = mixture.shape[0]
    flattened = mixture.reshape(features, -1).astype(jnp.float32)
    normed = layer_norm(flattened, out_gain[:, None], 0).astype(jnp.bfloat16)
    update = jnp.einsum("cx,cd->xd", normed, final_matrix, preferred_element_type=jnp.float32)
    result = pair_state.reshape(-1, features).astype(jnp.float32) + gating * update
    return result.astype(jnp.bfloat16).reshape(pair_state.shape)


def exchange_kernel(plan, sizes, opened, *refs):
    halves, inner, chans, subs = sizes
    cols = chans * subs
    block = inner * cols
    count = len(plan)
    sources, targets = refs[:count], refs[count : 2 * count]
    sems = refs[2 * count : 5 * count]
    opens = targets
    if opened:
        targets = refs[5 * count : 6 * count]
    row = lax.axis_index("dap")
    col = lax.axis_index("chan") * subs + lax.axis_index("sub")
    mine = lax.rem(row, inner) * cols + col
    half = row // inner
    whole = halves * block
    me = row * cols + col

    def place(q):
        owner_row, owner_col = q // cols, lax.rem(q, cols)
        return {"dap": owner_row, "chan": owner_col // subs, "sub": lax.rem(owner_col, subs)}

    barrier = pltpu.get_barrier_semaphore()
    everyone = any(spans for _, spans in plan)
    reach = whole if everyone else block
    for off in range(1, reach):
        q = lax.rem(me + off, whole) if everyone else half * block + lax.rem(mine + off, block)
        pl.semaphore_signal(barrier, inc=1, device_id=place(q), device_id_type=pl.DeviceIdType.MESH)
    pl.semaphore_wait(barrier, reach - 1)

    started = []
    for off in [0, *range(cols, reach), *range(1, cols)]:
        for (varies, spans), source, target, (sent, got, kept) in zip(
            plan, sources, targets, [sems[3 * n : 3 * n + 3] for n in range(count)]
        ):
            if spans:
                q = lax.rem(me + off, whole)
                slot, back = me, lax.rem(me - off + whole, whole)
            elif off < block:
                q = half * block + lax.rem(mine + off, block)
                slot, back = mine, lax.rem(mine - off + block, block)
            else:
                continue
            piece = source.at[q if varies else lax.rem(q, block)]
            if off == 0:
                copy = pltpu.make_async_copy(piece, target.at[slot], kept)
                copy.start()
                started.append((copy, None))
                continue
            copy = pltpu.make_async_remote_copy(
                src_ref=piece,
                dst_ref=target.at[slot],
                send_sem=sent.at[off],
                recv_sem=got.at[off],
                device_id=place(q),
                device_id_type=pl.DeviceIdType.MESH,
            )
            copy.start()
            if opened:
                started.append((copy, copy))
                continue
            arriving = pltpu.make_async_remote_copy(
                src_ref=piece,
                dst_ref=target.at[back],
                send_sem=sent.at[off],
                recv_sem=got.at[off],
                device_id=place(q),
                device_id_type=pl.DeviceIdType.MESH,
            )
            started.append((copy, arriving))
    if not opened:
        for copy, arriving in started:
            if arriving is None:
                copy.wait()
            else:
                copy.wait_send()
                arriving.wait_recv()
        return

    def unfold(target, open_ref, slot):
        rows, width = open_ref.shape[2:]
        open_ref[slot] = target[slot].reshape(target.shape[1], rows, width)

    for (varies, spans), source, target, open_ref, (sent, got, kept) in zip(
        plan, sources, targets, opens, [sems[3 * n : 3 * n + 3] for n in range(count)]
    ):
        slots = whole if spans else block
        base = me if spans else mine
        pltpu.make_async_copy(source.at[me if varies else mine], target.at[base], kept).wait()
        unfold(target, open_ref, base)

        def arrive(step, carry, slots=slots, base=base, source=source, target=target,
                   open_ref=open_ref, sent=sent, got=got):
            off = lax.rem(step + cols - 2, slots - 1) + 1
            back = lax.rem(base - off + slots, slots)
            arriving = pltpu.make_async_remote_copy(
                src_ref=source.at[0],
                dst_ref=target.at[back],
                send_sem=sent.at[off],
                recv_sem=got.at[off],
                device_id=place(back if slots == whole else half * block + back),
                device_id_type=pl.DeviceIdType.MESH,
            )
            arriving.wait_recv()
            unfold(target, open_ref, back)
            return carry

        lax.fori_loop(1, slots, arrive, 0)
    for copy, arriving in started:
        if arriving is not None:
            copy.wait_send()


def fold_kernel(spans, sizes, source, target, sent, got, kept, flat):
    halves, inner, chans, subs = sizes
    cols = chans * subs
    block = inner * cols
    slots = halves * block if spans else block
    row = lax.axis_index("dap")
    col = lax.axis_index("chan") * subs + lax.axis_index("sub")
    first = 0 if spans else (row // inner) * block
    base = row * cols + col - first

    def place(q):
        owner_row, owner_col = (first + q) // cols, lax.rem(q, cols)
        return {"dap": owner_row, "chan": owner_col // subs, "sub": lax.rem(owner_col, subs)}

    def push(off, slot):
        q = lax.rem(base + off, slots)
        return pltpu.make_async_remote_copy(
            src_ref=flat.at[q],
            dst_ref=target.at[slot],
            send_sem=sent.at[off],
            recv_sem=got.at[off],
            device_id=place(q),
            device_id_type=pl.DeviceIdType.MESH,
        )

    def fold(q):
        flat[q] = source[q].reshape(flat.shape[1:])

    barrier = pltpu.get_barrier_semaphore()
    for off in range(1, slots):
        pl.semaphore_signal(
            barrier,
            inc=1,
            device_id=place(lax.rem(base + off, slots)),
            device_id_type=pl.DeviceIdType.MESH,
        )
    pl.semaphore_wait(barrier, slots - 1)

    def send(step, carry):
        off = lax.rem(step + cols - 2, slots - 1) + 1
        fold(lax.rem(base + off, slots))
        push(off, base).start()
        return carry

    lax.fori_loop(1, slots, send, 0)
    fold(base)
    own = pltpu.make_async_copy(flat.at[base], target.at[base], kept)
    own.start()

    def finish_off(off, carry):
        copy = push(off, lax.rem(base - off + slots, slots))
        copy.wait_send()
        copy.wait_recv()
        return carry

    lax.fori_loop(1, slots, finish_off, 0)
    own.wait()


def fold_exchange(spans, sizes, number, array):
    slots, depth, rows, width = array.shape
    flat = (slots, depth, rows * width)
    return pl.pallas_call(
        functools.partial(fold_kernel, spans, sizes),
        out_shape=jax.ShapeDtypeStruct(flat, array.dtype),
        in_specs=[pl.BlockSpec(memory_space=pltpu.VMEM)],
        out_specs=pl.BlockSpec(memory_space=pl.ANY),
        scratch_shapes=[
            pltpu.SemaphoreType.DMA((slots,)),
            pltpu.SemaphoreType.DMA((slots,)),
            pltpu.SemaphoreType.DMA,
            pltpu.VMEM(flat, array.dtype),
        ],
        compiler_params=pltpu.CompilerParams(
            collective_id=number, has_side_effects=True, vmem_limit_bytes=24 * 2**20
        ),
    )(array)


def exchange(plan, sizes, number, *arrays, opened=None):
    halves, inner, chans, subs = sizes
    block = inner * chans * subs
    shapes, sems, landing = [], [], []
    for (varies, spans), array in zip(plan, arrays):
        slots = halves * block if spans else block
        if opened:
            shapes.append(jax.ShapeDtypeStruct((slots, array.shape[1]) + opened, array.dtype))
            landing.append(pltpu.VMEM((slots,) + array.shape[1:], array.dtype))
        else:
            shapes.append(jax.ShapeDtypeStruct((slots,) + array.shape[1:], array.dtype))
        sems += [
            pltpu.SemaphoreType.DMA((slots,)),
            pltpu.SemaphoreType.DMA((slots,)),
            pltpu.SemaphoreType.DMA,
        ]
    return pl.pallas_call(
        functools.partial(exchange_kernel, plan, sizes, opened is not None),
        out_shape=shapes,
        in_specs=[pl.BlockSpec(memory_space=pl.ANY)] * len(arrays),
        out_specs=[pl.BlockSpec(memory_space=pltpu.VMEM if opened else pl.ANY)] * len(arrays),
        scratch_shapes=sems + landing,
        compiler_params=pltpu.CompilerParams(
            collective_id=number,
            has_side_effects=True,
            vmem_limit_bytes=24 * 2**20 if opened else None,
        ),
    )(*arrays)


def product_kernel(turned, left_ref, right_ref, out_ref):
    left_tall, cols, depth, rows, width = left_ref.shape
    right_tall = right_ref.shape[0]

    def matrix(ref, tall, channel):
        return jnp.concatenate(
            [
                jnp.concatenate([ref[t, x, channel] for x in range(cols)], axis=1)
                for t in range(tall)
            ],
            axis=0,
        )

    side = 0 if turned else 1
    for channel in range(depth):
        mixed = lax.dot_general(
            matrix(left_ref, left_tall, channel),
            matrix(right_ref, right_tall, channel),
            (((side,), (side,)), ((), ())),
            preferred_element_type=jnp.float32,
        ).astype(out_ref.dtype)
        for t in range(out_ref.shape[0]):
            for x in range(cols):
                out_ref[t, x, channel] = mixed[
                    t * rows : (t + 1) * rows, x * width : (x + 1) * width
                ]


def product(turned, left, right):
    left_tall, cols, depth, rows, width = left.shape
    right_tall = right.shape[0]
    tall = cols if turned else left_tall
    step = 4 if depth % 4 == 0 else 1

    def spec(high):
        return pl.BlockSpec((high, cols, step, rows, width), lambda n: (0, 0, n, 0, 0))

    flops = 2 * depth * (tall * rows) * (cols * width) * (left_tall * rows if turned else cols * width)
    return pl.pallas_call(
        functools.partial(product_kernel, turned),
        out_shape=jax.ShapeDtypeStruct((tall, cols, depth, rows, width), jnp.bfloat16),
        grid=(depth // step,),
        in_specs=[spec(left_tall), spec(right_tall)],
        out_specs=spec(tall),
        compiler_params=pltpu.CompilerParams(vmem_limit_bytes=24 * 2**20),
        cost_estimate=pl.CostEstimate(
            flops=flops, bytes_accessed=2 * (left.size + right.size), transcendentals=0
        ),
    )(left, right)


def direct_shards(
    sizes,
    pair_input,
    first_gain,
    first_project,
    first_gate,
    first_norm,
    first_final,
    second_gain,
    second_project,
    second_gate,
    second_norm,
    second_final,
):
    halves, inner, chans, subs = sizes
    cols = chans * subs
    block = inner * cols
    rows, width, features = pair_input.shape
    depth = features // block
    span = rows * width

    def blocks(part):
        return part.reshape(-1, depth, span)

    def grid(received, tall):
        return received.reshape(tall, cols, depth, rows, width)

    left, right, gating = project_in(pair_input, first_gain, first_project, first_gate)
    left, right = exchange(
        ((False, False), (False, True)), sizes, 0, blocks(left), blocks(right),
        opened=(rows, width),
    )
    mixture = product(False, grid(left, inner), grid(right, halves * inner))
    mixture = fold_exchange(False, sizes, 1, mixture.reshape(-1, depth, rows, width))
    middle = finish(
        pair_input, mixture.reshape(features, span), gating, first_norm, first_final
    )
    left, right, gating = project_in(middle, second_gain, second_project, second_gate)
    left, right = exchange(
        ((False, False), (False, False)), sizes, 2, blocks(left), blocks(right),
        opened=(rows, width),
    )
    mixture = product(True, grid(left, inner), grid(right, inner))
    mixture = fold_exchange(True, sizes, 3, mixture.reshape(-1, depth, rows, width))
    mixture = mixture.reshape(halves, features, span)
    mixture = sum(mixture[n].astype(jnp.float32) for n in range(halves))
    return finish(middle, mixture, gating, second_norm, second_final)


def shards(
    pair_input,
    first_gain,
    first_project,
    first_gate,
    first_norm,
    first_final,
    second_gain,
    second_project,
    second_gate,
    second_norm,
    second_final,
):
    left_part, right_part, gating = project_in(pair_input, first_gain, first_project, first_gate)
    left_part, right_part = (
        lax.all_to_all(left_part, ("chan", "sub"), split_axis=0, concat_axis=2, tiled=True),
        lax.all_to_all(right_part, ("chan", "sub"), split_axis=0, concat_axis=2, tiled=True),
    )
    mixture = jnp.einsum(
        "cik,cjk->cij",
        left_part,
        lax.all_gather(right_part, "dap", axis=1, tiled=True),
        preferred_element_type=jnp.float32,
    ).astype(jnp.bfloat16)
    mixture = lax.all_to_all(mixture, ("chan", "sub"), split_axis=2, concat_axis=0, tiled=True)
    middle = finish(pair_input, mixture, gating, first_norm, first_final)
    left_part, right_part, gating = project_in(middle, second_gain, second_project, second_gate)
    left_part, right_part = (
        lax.all_to_all(left_part, ("chan", "sub"), split_axis=0, concat_axis=2, tiled=True),
        lax.all_to_all(right_part, ("chan", "sub"), split_axis=0, concat_axis=2, tiled=True),
    )
    turned = lax.all_to_all(left_part, "dap", split_axis=2, concat_axis=1, tiled=True)
    mixture = jnp.einsum(
        "cki,ckj->cij",
        turned,
        lax.all_gather(right_part, "dap", axis=1, tiled=True),
        preferred_element_type=jnp.float32,
    )
    mixture = lax.all_to_all(
        mixture.astype(jnp.bfloat16), ("chan", "sub"), split_axis=2, concat_axis=0, tiled=True
    )
    return finish(middle, mixture, gating, second_norm, second_final)


def solution(mesh):
    placed = (
        P(("groups", "dap"), ("chan", "sub"), None),
        P(),
        P(),
        P(),
        P(),
        P(),
        P(),
        P(),
        P(),
        P(),
        P(),
    )
    chans, subs, rows = mesh.shape["chan"], mesh.shape["sub"], mesh.shape["dap"]
    halves = 2 if rows % 2 == 0 else 1
    sizes = (halves, rows // halves, chans, subs)
    direct = functools.partial(direct_shards, sizes)

    def chosen(pair_input, *weights):
        features = pair_input.shape[2]
        square = pair_input.shape[0] == pair_input.shape[1] and rows == chans * subs
        if square and features % (16 * (rows // halves) * chans * subs) == 0:
            return direct(pair_input, *weights)
        return shards(pair_input, *weights)

    return jax.shard_map(
        chosen,
        mesh=mesh,
        in_specs=placed,
        out_specs=P(("groups", "dap"), ("chan", "sub"), None),
        check_vma=False,
    )
```
